32 devices in a mesh: ctx: 8 (over z, x), tp: 4 (over y, core).
Axes of the slice: x: 2, y: 2, z: 4, core: 2. Of those that a mesh axis runs over, the one named last changes fastest.
Arguments:
- tokens: bfloat16 [8192, 4096], P(('ctx', 'tp')), may hold values from -21 to 21
- segment: int32 [8192], P('ctx'), may hold values from 0 to 1, never falling along the last dimension, each value on 1 to 4608 neighbouring positions
- w_feat_q: bfloat16 [4096, 512], P(None, 'tp'), may hold values from -0.09375 to 0.09375
- w_feat_k: bfloat16 [4096, 512], P(None, 'tp'), may hold values from -0.09375 to 0.09375
- w_query: bfloat16 [4096, 4096], P(None, 'tp'), may hold values from -0.09375 to 0.09375
- w_key: bfloat16 [4096, 4096], P(None, 'tp'), may hold values from -0.09375 to 0.09375
- w_value: bfloat16 [4096, 4096], P(None, 'tp'), may hold values from -0.09375 to 0.09375
- w_out: bfloat16 [4096, 4096], P('tp'), may hold values from -0.09375 to 0.09375
Outputs:
- layer_out: bfloat16 [8192, 4096], P(('ctx', 'tp'))
The draws below stay inside these ranges and needn't reach their ends.
Inputs may be any that keep to these rules, and one draw needn't show every extreme that they name: `segment`: never falls along the sequence; 2 documents, each of 1 to 4608 tokens, one of exactly 4608.
All inputs are finite; a program needn't handle non-finite values.
Results may differ from the reference program's by a relative error of at most 0.006.
The reference program's roundings to bfloat16 on the way (of `mixed`) count: a program that leaves them out, or rounds other values in their place, can miss the bound.
Values may be sent and summed in bfloat16 or wider, within the bound.
A program may use at most 192 MiB of HBM per device.

```python
import math
import jax
import jax.numpy as jnp
import numpy as np
from jax import lax

D = 4096
HEADS = 32
HEAD_DIM = 128
FEAT = 16
WINDOW = 64
TOK_DEV = 1024
TAYLOR = 273
TOKENS = 8192
DOCS = 2
DOC_MOST = 4608


def draw_tokens(key, part):
    key_value = jax.random.fold_in(key, 1)
    values = jnp.clip(jax.random.normal(key_value, (TOKENS, D), jnp.float32), -6.0, 6.0)
    return values.astype(jnp.bfloat16)


def block_scale(stream_key, shape, shards, low, largest):
    factor_of, own = 1.0, jax.random.fold_in(stream_key, 6)
    for dim, shards_of in shards:
        draws = jnp.exp(jax.random.uniform(jax.random.fold_in(own, dim), (shards_of,), jnp.float32, low / len(shards), largest / len(shards)))
        factor_of = factor_of * jnp.repeat(draws, shape[dim] // shards_of).reshape([-1 if axis == dim else 1 for axis in range(len(shape))])
    return factor_of


def split_up(amount, total, reach, lean):
    loads = [(1 << 20) // math.isqrt(standing ** lean) + 1 for standing in range(2, amount + 1)]
    spare, given = total - reach - (amount - 1), [1] * (amount - 1)
    while spare > 0:
        movable = [i for i in range(amount - 1) if given[i] < reach]
        pool, budget = sum([loads[i] for i in movable]), spare
        for i in movable:
            addition = min(reach - given[i], max(1, budget * loads[i] // pool), spare)
            given[i] = given[i] + addition
            spare = spare - addition
    return np.array([reach] + given)


def ragged(rng, count, total, reach, skew):
    if count == 2:
        one = jax.random.randint(rng, (), max(1, total - reach), min(reach, total - 1) + 1)
        return jnp.stack([one, total - one])
    tallies = jnp.asarray(split_up(count, total, reach, skew), jnp.int32)
    pairs = (count - 1) // 2
    source_of, sink = tallies[1:1 + 2 * pairs:2], tallies[2:2 + 2 * pairs:2]
    slack = jnp.minimum(source_of - 1, reach - sink)
    shifted = jax.random.randint(jax.random.fold_in(rng, 1), (pairs,), 0, 1 << 20) % (slack + 1)
    tallies = tallies.at[1:1 + 2 * pairs:2].set(source_of - shifted).at[2:2 + 2 * pairs:2].set(sink + shifted)
    return tallies[jax.random.permutation(jax.random.fold_in(rng, 2), count)]


def normal_values(own_key, dims, scale, reach, pieces=(), kind=jnp.bfloat16):
    values = jax.random.normal(own_key, dims, jnp.float32) * scale
    if len(pieces) > 0:
        values = block_scale(own_key, dims, pieces, -0.22, 0.18) * values
    return jnp.clip(values, min=-reach, max=reach).astype(kind)


def setup_inputs(seed: int = 0) -> dict:
    key_list = jax.random.split(jax.random.key(seed), 9)
    return {
        "tokens": draw_tokens(jax.random.fold_in(key_list[8], 71), 0),
        "segment": jnp.searchsorted(jnp.cumsum(ragged(key_list[1], DOCS, TOKENS, DOC_MOST, 1)), jnp.arange(TOKENS), side="right").astype(jnp.int32),
        "w_feat_q": normal_values(key_list[2], (D, HEADS * FEAT), D ** -0.5, 0.09375, ((1, 4),)),
        "w_feat_k": normal_values(key_list[3], (D, HEADS * FEAT), D ** -0.5, 0.09375, ((1, 4),)),
        "w_query": normal_values(key_list[4], (D, HEADS * HEAD_DIM), D ** -0.5, 0.09375, ((1, 4),)),
        "w_key": normal_values(key_list[5], (D, HEADS * HEAD_DIM), D ** -0.5, 0.09375, ((1, 4),)),
        "w_value": normal_values(key_list[6], (D, HEADS * HEAD_DIM), D ** -0.5, 0.09375, ((1, 4),)),
        "w_out": normal_values(key_list[7], (HEADS * HEAD_DIM, D), (HEADS * HEAD_DIM) ** -0.5, 0.09375, ((0, 4),)),
    }


HIGH = lax.Precision.HIGHEST


def taylor_map(values):
    width = values.shape[-1]
    square = (values[..., :, None] * values[..., None, :]).reshape(values.shape[:-1] + (width * width,))
    ones = jnp.ones(values.shape[:-1] + (1,), values.dtype)
    return jnp.concatenate([ones, values * width ** -0.25, square * (0.5 ** 0.5 / width ** 0.5)], axis=-1)


def heads_of(tokens, weight, width):
    total = tokens.shape[0]
    projected = jnp.dot(tokens, weight, preferred_element_type=jnp.float32).astype(jnp.bfloat16)
    projected = lax.optimization_barrier(projected)
    return projected.astype(jnp.float32).reshape(total, -1, width).transpose(1, 0, 2)


def reference(tokens, segment, w_feat_q, w_feat_k, w_query, w_key, w_value, w_out):
    feat_q = heads_of(tokens, w_feat_q, FEAT)
    feat_k = heads_of(tokens, w_feat_k, FEAT)
    query_w = heads_of(tokens, w_query, HEAD_DIM)
    key_w = heads_of(tokens, w_key, HEAD_DIM)
    value = heads_of(tokens, w_value, HEAD_DIM)
    block = min(512, TOK_DEV)
    count = TOKENS // block

    def blocked(array):
        return array.reshape(HEADS, count, block, array.shape[-1]).transpose(1, 0, 2, 3)

    seg_blocks = segment.reshape(count, block)
    init = (jnp.zeros((HEADS, TAYLOR, HEAD_DIM), jnp.float32), jnp.zeros((HEADS, TAYLOR), jnp.float32),
            jnp.array(-1, jnp.int32), jnp.zeros((HEADS, WINDOW, HEAD_DIM), jnp.float32),
            jnp.zeros((HEADS, WINDOW, HEAD_DIM), jnp.float32), jnp.full((WINDOW,), -1, jnp.int32))

    def advance(carry, inputs):
        state, normal, last_seg, tail_key, tail_value, tail_seg = carry
        query_f, key_f, query_n, key_n, values, seg = inputs
        rows = jnp.arange(block)
        allowed = (seg[:, None] == seg[None, :]) & (rows[None, :] <= rows[:, None])
        inner = jnp.einsum('hsf,htf->hst', query_f, key_f, precision=HIGH) / FEAT ** 0.5
        kernel = jnp.where(allowed[None], 1.0 + inner + 0.5 * inner * inner, 0.0)
        numerator = jnp.einsum('hst,htd->hsd', kernel, values, precision=HIGH)
        denominator = jnp.sum(kernel, axis=-1)
        mapped_q = taylor_map(query_f)
        carried = (seg == last_seg)[None, :]
        numerator = numerator + jnp.where(carried[..., None], jnp.einsum('hsf,hfd->hsd', mapped_q, state, precision=HIGH), 0.0)
        denominator = denominator + jnp.where(carried, jnp.einsum('hsf,hf->hs', mapped_q, normal, precision=HIGH), 0.0)
        linear_part = numerator / denominator[..., None]
        key_rows = jnp.concatenate([tail_key, key_n], axis=1)
        value_rows = jnp.concatenate([tail_value, values], axis=1)
        key_seg = jnp.concatenate([tail_seg, seg])
        columns = jnp.arange(WINDOW + block)
        near = (columns[None, :] <= rows[:, None] + WINDOW) & (columns[None, :] > rows[:, None])
        visible = near & (key_seg[None, :] == seg[:, None])
        scores = jnp.einsum('hsd,htd->hst', query_n, key_rows, precision=HIGH) / HEAD_DIM ** 0.5
        scores = jnp.where(visible[None], scores, -jnp.inf)
        peak = jnp.max(scores, axis=-1, keepdims=True)
        expo = jnp.exp(scores - peak)
        window_part = jnp.einsum('hst,htd->hsd', expo, value_rows, precision=HIGH) / jnp.sum(expo, axis=-1)[..., None]
        mixed = (linear_part + window_part).astype(jnp.bfloat16)
        mapped_k = taylor_map(key_f) * (seg == seg[-1])[None, :, None].astype(jnp.float32)
        tail_state = jnp.einsum('htf,htd->hfd', mapped_k, values, precision=HIGH)
        tail_normal = jnp.sum(mapped_k, axis=1)
        keep = (seg[0] == seg[-1]) & (last_seg == seg[-1])
        state = tail_state + jnp.where(keep, state, 0.0)
        normal = tail_normal + jnp.where(keep, normal, 0.0)
        new_carry = (state, normal, seg[-1], key_rows[:, -WINDOW:], value_rows[:, -WINDOW:], key_seg[-WINDOW:])
        return new_carry, mixed

    final, mixed = lax.scan(advance, init, (blocked(feat_q), blocked(feat_k), blocked(query_w), blocked(key_w), blocked(value), seg_blocks))
    mixed = mixed.transpose(0, 2, 1, 3).reshape(TOKENS, HEADS * HEAD_DIM)
    return jnp.dot(mixed, w_out, preferred_element_type=jnp.float32).astype(jnp.bfloat16)
```

```python
import functools

import jax
import jax.numpy as jnp
import numpy as np
from jax import lax
from jax.experimental import pallas as pl
from jax.experimental.pallas import tpu as pltpu
from jax.sharding import PartitionSpec as P

HEAD_DIM = 128
FEAT = 16
WINDOW = 64
CORES = 2
ROWS = 160
MARK_LANE = 127
LOW_LANE = 64


def feature_tables(heads):
    first = np.zeros((heads, ROWS, heads * FEAT), np.float32)
    second = np.zeros((heads, ROWS, heads * FEAT), np.float32)
    rows = np.zeros((8, ROWS), np.float32)
    rows[0, 0] = rows[1, 0] = rows[2, 0] = 1.0
    for i in range(FEAT):
        rows[1, 1 + i] = 1.0
        rows[2, 1 + i] = 0.25
        for h in range(heads):
            first[h, 1 + i, h * FEAT + i] = 1.0
    at = 1 + FEAT
    for i in range(FEAT):
        for j in range(i, FEAT):
            rows[2, at] = 1.0 / 32 if i == j else 1.0 / 16
            for h in range(heads):
                first[h, at, h * FEAT + i] = 1.0
                second[h, at, h * FEAT + j] = 1.0
            at += 1
    return (
        jnp.asarray(first, jnp.bfloat16),
        jnp.asarray(second, jnp.bfloat16),
        jnp.asarray(rows),
        jnp.asarray(np.ascontiguousarray(rows.T)),
    )


def dot_last(a, b):
    return lax.dot_general(a, b, (((1,), (1,)), ((), ())), preferred_element_type=jnp.float32)


def dot_f32(a, b):
    return jnp.dot(a, b, preferred_element_type=jnp.float32)


def state_kernel(heads, fk, v, seg_row, last, first, second, cols, out):
    h = pl.program_id(0)
    keep = (seg_row[...] == last[:, :1]).astype(jnp.float32)
    a = dot_last(first[0], fk[...]) + cols[:, 0:1]
    b = dot_last(second[0], fk[...]) + cols[:, 1:2]
    phi = (a * b * keep).astype(jnp.bfloat16)
    out[pl.ds(h, 1)] = dot_f32(phi, v[...]).astype(jnp.bfloat16)[None]
    normal = jnp.sum(phi.astype(jnp.float32), axis=1, keepdims=True)
    high = normal.astype(jnp.bfloat16).astype(jnp.float32)
    low = normal - high
    lane = lax.broadcasted_iota(jnp.int32, (ROWS, HEAD_DIM), 1)
    row = lax.broadcasted_iota(jnp.int32, (ROWS, HEAD_DIM), 0)

    @pl.when(h == 0)
    def _():
        mark = jnp.where((row == ROWS - 1) & (lane == MARK_LANE), last[:, :1], 0.0)
        out[heads] = mark.astype(jnp.bfloat16)

    add = jnp.where(lane == h, high, jnp.where(lane == h + LOW_LANE, low, 0.0))
    out[heads] = (out[heads].astype(jnp.float32) + add).astype(jnp.bfloat16)


def mix_kernel(
    fq, fk, q, k, v, tail_k, tail_v, seg_col, seg_row, key_seg, carried, state, normal,
    first, second, rows, out,
):
    h = pl.program_id(0)
    tokens, width = fq.shape
    lane = lax.broadcasted_iota(jnp.int32, (1, width), 1)
    mine = ((lane >= h * FEAT) & (lane < (h + 1) * FEAT)).astype(jnp.float32)
    fk_head = fk[...] * mine.astype(jnp.bfloat16)
    fq_all = fq[...]
    fq_scaled = fq_all * jnp.asarray(0.25, jnp.bfloat16)
    value = jnp.concatenate([v[...], jnp.ones((tokens, HEAD_DIM), jnp.bfloat16)], axis=1)
    tail = jnp.concatenate([tail_v[...], jnp.ones((WINDOW, HEAD_DIM), jnp.bfloat16)], axis=1)

    state_lane = lax.broadcasted_iota(jnp.int32, (ROWS, HEAD_DIM), 1)
    column = jnp.sum(jnp.where(state_lane == h, normal[...], 0.0), axis=1, keepdims=True)
    joint = jnp.concatenate([state[0], jnp.broadcast_to(column, (ROWS, HEAD_DIM))], axis=1)
    joint_high = joint.astype(jnp.bfloat16)
    joint_low = (joint - joint_high.astype(jnp.float32)).astype(jnp.bfloat16)

    block = min(256, tokens)
    for begin in range(0, tokens, block):
        finish = begin + block
        seg_here = seg_col[begin:finish]
        a = dot_last(fq_all[begin:finish], first[0]) + rows[0:1]
        b = dot_last(fq_all[begin:finish], second[0]) + rows[1:2]
        phi = (a * b * rows[2:3]).astype(jnp.bfloat16)
        entering = dot_f32(phi, joint_high) + dot_f32(phi, joint_low)
        total = jnp.where(seg_here == carried[:, :1], entering, 0.0)
        if begin:
            inner = dot_last(fq_scaled[begin:finish], fk_head[:begin]) + 1.0
            kernel = jnp.where(
                seg_here == seg_row[:, :begin], 0.5 * (inner * inner) + 0.5, 0.0
            )
            total = total + dot_f32(kernel.astype(jnp.bfloat16), value[:begin])
        inner = dot_last(fq_scaled[begin:finish], fk_head[begin:finish]) + 1.0
        row_at = lax.broadcasted_iota(jnp.int32, (block, block), 0)
        col_at = lax.broadcasted_iota(jnp.int32, (block, block), 1)
        kernel = jnp.where(
            (seg_here == seg_row[:, begin:finish]) & (col_at <= row_at),
            0.5 * (inner * inner) + 0.5,
            0.0,
        )
        total = total + dot_f32(kernel.astype(jnp.bfloat16), value[begin:finish])
        linear = total[:, :HEAD_DIM] / total[:, HEAD_DIM:]

        small = min(128, block)
        for start in range(begin, finish, small):
            stop = start + small
            if start:
                keys, values = k[start - WINDOW : stop], value[start - WINDOW : stop]
            else:
                keys = jnp.concatenate([tail_k[...], k[:stop]], axis=0)
                values = jnp.concatenate([tail, value[:stop]], axis=0)
            scores = dot_last(q[start:stop], keys) * (1.4426950408889634 / HEAD_DIM**0.5)
            row_at = lax.broadcasted_iota(jnp.int32, (small, small + WINDOW), 0)
            col_at = lax.broadcasted_iota(jnp.int32, (small, small + WINDOW), 1)
            near = (col_at <= row_at + WINDOW) & (col_at > row_at)
            same = key_seg[:, start : stop + WINDOW] == seg_col[start:stop] + 1.0
            scores = jnp.where(near & same, scores, -jnp.inf)
            peak = jnp.max(scores, axis=1, keepdims=True)
            expo = jnp.exp2(scores - peak).astype(jnp.bfloat16)
            near_sum = dot_f32(expo, values)
            part = near_sum[:, :HEAD_DIM] / near_sum[:, HEAD_DIM:]
            out[start:stop] = (linear[start - begin : stop - begin] + part).astype(jnp.bfloat16)


def whole(shape):
    return pl.BlockSpec(shape, lambda h: (0,) * len(shape))


def own_state(fk, v, seg_row, last, tables):
    tokens, width = fk.shape
    heads = v.shape[1] // HEAD_DIM
    first, second, _, cols = tables
    per_head = pl.BlockSpec((1, ROWS, width), lambda h: (h, 0, 0))
    return pl.pallas_call(
        functools.partial(state_kernel, heads),
        grid=(heads,),
        in_specs=[
            whole((tokens, width)),
            pl.BlockSpec((tokens, HEAD_DIM), lambda h: (0, h)),
            whole((1, tokens)),
            whole((1, HEAD_DIM)),
            per_head,
            per_head,
            whole((ROWS, 8)),
        ],
        out_specs=whole((heads + 1, ROWS, HEAD_DIM)),
        out_shape=jax.ShapeDtypeStruct((heads + 1, ROWS, HEAD_DIM), jnp.bfloat16),
        compiler_params=pltpu.CompilerParams(vmem_limit_bytes=32 << 20),
        cost_estimate=pl.CostEstimate(
            flops=2 * heads * ROWS * tokens * 384, bytes_accessed=4 << 20, transcendentals=0
        ),
        name="own_state",
    )(fk, v, seg_row, last, first, second, cols)


def mix(fq, fk, q, k, v, tail, seg_col, seg_row, key_seg, carried, state, normal, tables):
    tokens, width = fk.shape
    heads = v.shape[1] // HEAD_DIM
    first, second, rows, _ = tables
    per_head = pl.BlockSpec((1, ROWS, width), lambda h: (h, 0, 0))
    wide = pl.BlockSpec((tokens, HEAD_DIM), lambda h: (0, h))
    return pl.pallas_call(
        mix_kernel,
        grid=(heads,),
        in_specs=[
            whole((tokens, width)),
            whole((tokens, width)),
            wide,
            wide,
            wide,
            pl.BlockSpec((WINDOW, HEAD_DIM), lambda h: (0, h)),
            pl.BlockSpec((WINDOW, HEAD_DIM), lambda h: (1, h)),
            whole((tokens, 1)),
            whole((1, tokens)),
            whole((1, tokens + WINDOW)),
            whole((1, HEAD_DIM)),
            pl.BlockSpec((1, ROWS, HEAD_DIM), lambda h: (h, 0, 0)),
            whole((ROWS, HEAD_DIM)),
            per_head,
            per_head,
            whole((8, ROWS)),
        ],
        out_specs=wide,
        out_shape=jax.ShapeDtypeStruct((tokens, heads * HEAD_DIM), jnp.bfloat16),
        compiler_params=pltpu.CompilerParams(vmem_limit_bytes=48 << 20),
        cost_estimate=pl.CostEstimate(
            flops=heads * tokens * tokens * 768,
            bytes_accessed=10 << 20,
            transcendentals=heads * tokens * 192,
        ),
        name="mix",
    )(
        fq, fk, q, k, v, tail, tail, seg_col, seg_row, key_seg, carried, state, normal,
        first, second, rows,
    )


def body(tokens, segment, w_feat_q, w_feat_k, w_query, w_key, w_value, w_out):
    group = lax.axis_size("tp")
    chips = group // CORES
    ranges = lax.axis_size("ctx")
    place = lax.axis_index("ctx")
    me = lax.axis_index("tp")
    chip, core = me // CORES, me % CORES
    part = tokens.shape[0]
    pair_rows = CORES * part
    count = segment.shape[0]
    heads = w_value.shape[1] // HEAD_DIM
    tables = feature_tables(heads)

    swap = [(i, i ^ 1) for i in range(group)]

    def to_chip(block, distance):
        return lax.ppermute(
            block, "tp", [(i, (i + CORES * distance) % group) for i in range(group)]
        )

    onward = [(i, i + 1) for i in range(ranges - 1)]
    seg_float = segment.astype(jnp.float32)
    tail_mark = lax.ppermute(segment[-WINDOW:] + 1, "ctx", onward).astype(jnp.float32)
    last = seg_float[-1]
    seg_row, seg_col = seg_float[None, :], seg_float[:, None]
    key_seg = jnp.concatenate([tail_mark, seg_float + 1.0])[None, :]

    def pair_of(block):
        other = lax.ppermute(block, "tp", swap)
        low = jnp.where(core == 0, block, other)
        high = jnp.where(core == 0, other, block)
        return jnp.concatenate([low, high], axis=0)

    arriving = [to_chip(tokens, r) for r in range(1, chips)]
    pieces = [pair_of(tokens)] + [pair_of(block) for block in arriving]

    def project(weight):
        result = jnp.zeros((count, weight.shape[1]), jnp.bfloat16)
        for r, piece in enumerate(pieces):
            at = lax.rem(chip + chips - r, chips) * pair_rows
            rows = jnp.dot(piece, weight, preferred_element_type=jnp.float32)
            result = lax.dynamic_update_slice(result, rows.astype(jnp.bfloat16), (at, 0))
        return result

    value = project(w_value)
    feat_k = project(w_feat_k)
    key = project(w_key)
    last_lanes = jnp.full((1, HEAD_DIM), last)
    payload = own_state(feat_k, value, seg_row, last_lanes, tables)
    everything = lax.all_gather(payload, "ctx")
    tail = lax.ppermute(
        jnp.concatenate([key[-WINDOW:], value[-WINDOW:]], axis=0), "ctx", onward
    )
    query = project(w_query)
    feat_q = project(w_feat_q)

    marks = everything[:, heads, ROWS - 1, MARK_LANE].astype(jnp.float32)
    order = jnp.arange(ranges)
    carried = jnp.max(jnp.where(order < place, marks, -5.0))
    chosen = (order < place) & (marks == carried)
    summed = jnp.sum(
        jnp.where(chosen[:, None, None, None], everything.astype(jnp.float32), 0.0), axis=0
    )
    state = summed[:heads]
    normal = summed[heads, :, :LOW_LANE] + summed[heads, :, LOW_LANE:]
    normal = jnp.concatenate([normal, normal], axis=1)
    mixed = mix(
        feat_q, feat_k, query, key, value, tail, seg_col, seg_row, key_seg,
        jnp.full((1, HEAD_DIM), carried), state, normal, tables,
    )

    def partial_sum(to, which):
        rows = lax.dynamic_slice(
            mixed, (to * pair_rows + which * part, 0), (part, mixed.shape[1])
        )
        return jnp.dot(rows, w_out, preferred_element_type=jnp.float32)

    def chip_sum(to):
        given = lax.ppermute(partial_sum(to, 1 - core).astype(jnp.bfloat16), "tp", swap)
        return partial_sum(to, core) + given.astype(jnp.float32)

    received = []
    for r in range(1, chips):
        there = lax.rem(chip + r, chips)
        received.append(to_chip(chip_sum(there).astype(jnp.bfloat16), r))
    total = chip_sum(chip)
    for block in received:
        total = total + block.astype(jnp.float32)
    return total.astype(jnp.bfloat16)


def solution(mesh):
    in_specs = (
        P(("ctx", "tp"), None),
        P("ctx"),
        P(None, "tp"),
        P(None, "tp"),
        P(None, "tp"),
        P(None, "tp"),
        P(None, "tp"),
        P("tp", None),
    )
    out_specs = P(("ctx", "tp"), None)
    return jax.shard_map(body, mesh=mesh, in_specs=in_specs, out_specs=out_specs, check_vma=False)
```

```python
import functools

import jax
import jax.numpy as jnp
import numpy as np
from jax import lax
from jax.experimental import pallas as pl
from jax.experimental.pallas import tpu as pltpu
from jax.sharding import PartitionSpec as P

HEAD_DIM = 128
FEAT = 16
WINDOW = 64
CORES = 2
ROWS = 160
MARK_LANE = 127
LOW_LANE = 64


def feature_tables(heads):
    first = np.zeros((heads, ROWS, heads * FEAT), np.float32)
    second = np.zeros((heads, ROWS, heads * FEAT), np.float32)
    rows = np.zeros((8, ROWS), np.float32)
    rows[0, 0] = rows[1, 0] = rows[2, 0] = 1.0
    for i in range(FEAT):
        rows[1, 1 + i] = 1.0
        rows[2, 1 + i] = 0.25
        for h in range(heads):
            first[h, 1 + i, h * FEAT + i] = 1.0
    at = 1 + FEAT
    for i in range(FEAT):
        for j in range(i, FEAT):
            rows[2, at] = 1.0 / 32 if i == j else 1.0 / 16
            for h in range(heads):
                first[h, at, h * FEAT + i] = 1.0
                second[h, at, h * FEAT + j] = 1.0
            at += 1
    return (
        jnp.asarray(first, jnp.bfloat16),
        jnp.asarray(second, jnp.bfloat16),
        jnp.asarray(rows),
        jnp.asarray(np.ascontiguousarray(rows.T)),
    )


def dot_last(a, b):
    return lax.dot_general(a, b, (((1,), (1,)), ((), ())), preferred_element_type=jnp.float32)


def dot_f32(a, b):
    return jnp.dot(a, b, preferred_element_type=jnp.float32)


def state_kernel(heads, fk, v, seg_row, last, first, second, cols, out):
    h = pl.program_id(0)
    keep = (seg_row[...] == last[:, :1]).astype(jnp.float32)
    a = dot_last(first[0], fk[...]) + cols[:, 0:1]
    b = dot_last(second[0], fk[...]) + cols[:, 1:2]
    phi = (a * b * keep).astype(jnp.bfloat16)
    out[pl.ds(h, 1)] = dot_f32(phi, v[...]).astype(jnp.bfloat16)[None]
    normal = jnp.sum(phi.astype(jnp.float32), axis=1, keepdims=True)
    high = normal.astype(jnp.bfloat16).astype(jnp.float32)
    low = normal - high
    lane = lax.broadcasted_iota(jnp.int32, (ROWS, HEAD_DIM), 1)
    row = lax.broadcasted_iota(jnp.int32, (ROWS, HEAD_DIM), 0)

    @pl.when(h == 0)
    def _():
        mark = jnp.where((row == ROWS - 1) & (lane == MARK_LANE), last[:, :1], 0.0)
        out[heads] = mark.astype(jnp.bfloat16)

    add = jnp.where(lane == h, high, jnp.where(lane == h + LOW_LANE, low, 0.0))
    out[heads] = (out[heads].astype(jnp.float32) + add).astype(jnp.bfloat16)


def local_kernel(
    fq, fk, q, k, v, tail_k, tail_v, seg_col, seg_row, key_seg, sums, near_out,
):
    h = pl.program_id(0)
    tokens, width = fq.shape
    lane = lax.broadcasted_iota(jnp.int32, (1, width), 1)
    mine = ((lane >= h * FEAT) & (lane < (h + 1) * FEAT)).astype(jnp.float32)
    fk_head = fk[...] * mine.astype(jnp.bfloat16)
    fq_scaled = fq[...] * jnp.asarray(0.25, jnp.bfloat16)
    value = jnp.concatenate([v[...], jnp.ones((tokens, HEAD_DIM), jnp.bfloat16)], axis=1)
    tail = jnp.concatenate([tail_v[...], jnp.ones((WINDOW, HEAD_DIM), jnp.bfloat16)], axis=1)

    block = min(256, tokens)
    for begin in range(0, tokens, block):
        finish = begin + block
        seg_here = seg_col[begin:finish]
        total = None
        if begin:
            inner = dot_last(fq_scaled[begin:finish], fk_head[:begin]) + 1.0
            kernel = jnp.where(
                seg_here == seg_row[:, :begin], 0.5 * (inner * inner) + 0.5, 0.0
            )
            total = dot_f32(kernel.astype(jnp.bfloat16), value[:begin])
        inner = dot_last(fq_scaled[begin:finish], fk_head[begin:finish]) + 1.0
        row_at = lax.broadcasted_iota(jnp.int32, (block, block), 0)
        col_at = lax.broadcasted_iota(jnp.int32, (block, block), 1)
        kernel = jnp.where(
            (seg_here == seg_row[:, begin:finish]) & (col_at <= row_at),
            0.5 * (inner * inner) + 0.5,
            0.0,
        )
        here = dot_f32(kernel.astype(jnp.bfloat16), value[begin:finish])
        sums[begin:finish] = here if total is None else total + here

        small = min(128, block)
        for start in range(begin, finish, small):
            stop = start + small
            if start:
                keys, values = k[start - WINDOW : stop], value[start - WINDOW : stop]
            else:
                keys = jnp.concatenate([tail_k[...], k[:stop]], axis=0)
                values = jnp.concatenate([tail, value[:stop]], axis=0)
            scores = dot_last(q[start:stop], keys) * (1.4426950408889634 / HEAD_DIM**0.5)
            row_at = lax.broadcasted_iota(jnp.int32, (small, small + WINDOW), 0)
            col_at = lax.broadcasted_iota(jnp.int32, (small, small + WINDOW), 1)
            near = (col_at <= row_at + WINDOW) & (col_at > row_at)
            same = key_seg[:, start : stop + WINDOW] == seg_col[start:stop] + 1.0
            scores = jnp.where(near & same, scores, -jnp.inf)
            peak = jnp.max(scores, axis=1, keepdims=True)
            expo = jnp.exp2(scores - peak).astype(jnp.bfloat16)
            near_sum = dot_f32(expo, values)
            part = near_sum[:, :HEAD_DIM] / near_sum[:, HEAD_DIM:]
            near_out[start:stop] = part


def carry_kernel(fq, seg_col, carried, state, normal, first, second, rows, sums, near_in, out):
    h = pl.program_id(0)
    tokens = fq.shape[0]
    state_lane = lax.broadcasted_iota(jnp.int32, (ROWS, HEAD_DIM), 1)
    column = jnp.sum(jnp.where(state_lane == h, normal[...], 0.0), axis=1, keepdims=True)
    joint = jnp.concatenate([state[0], jnp.broadcast_to(column, (ROWS, HEAD_DIM))], axis=1)
    joint_high = joint.astype(jnp.bfloat16)
    joint_low = (joint - joint_high.astype(jnp.float32)).astype(jnp.bfloat16)
    block = min(256, tokens)
    for begin in range(0, tokens, block):
        finish = begin + block
        a = dot_last(fq[begin:finish], first[0]) + rows[0:1]
        b = dot_last(fq[begin:finish], second[0]) + rows[1:2]
        phi = (a * b * rows[2:3]).astype(jnp.bfloat16)
        entering = dot_f32(phi, joint_high) + dot_f32(phi, joint_low)
        total = sums[begin:finish] + jnp.where(
            seg_col[begin:finish] == carried[:, :1], entering, 0.0
        )
        linear = total[:, :HEAD_DIM] / total[:, HEAD_DIM:]
        out[begin:finish] = (linear + near_in[begin:finish]).astype(jnp.bfloat16)


def whole(shape):
    return pl.BlockSpec(shape, lambda h: (0,) * len(shape))


def own_state(fk, v, seg_row, last, tables):
    tokens, width = fk.shape
    heads = v.shape[1] // HEAD_DIM
    first, second, _, cols = tables
    per_head = pl.BlockSpec((1, ROWS, width), lambda h: (h, 0, 0))
    return pl.pallas_call(
        functools.partial(state_kernel, heads),
        grid=(heads,),
        in_specs=[
            whole((tokens, width)),
            pl.BlockSpec((tokens, HEAD_DIM), lambda h: (0, h)),
            whole((1, tokens)),
            whole((1, HEAD_DIM)),
            per_head,
            per_head,
            whole((ROWS, 8)),
        ],
        out_specs=whole((heads + 1, ROWS, HEAD_DIM)),
        out_shape=jax.ShapeDtypeStruct((heads + 1, ROWS, HEAD_DIM), jnp.bfloat16),
        compiler_params=pltpu.CompilerParams(vmem_limit_bytes=32 << 20),
        cost_estimate=pl.CostEstimate(
            flops=2 * heads * ROWS * tokens * 384, bytes_accessed=4 << 20, transcendentals=0
        ),
        name="own_state",
    )(fk, v, seg_row, last, first, second, cols)


def mix_local(fq, fk, q, k, v, tail, seg_col, seg_row, key_seg):
    tokens, width = fk.shape
    heads = v.shape[1] // HEAD_DIM
    wide = pl.BlockSpec((tokens, HEAD_DIM), lambda h: (0, h))
    double = pl.BlockSpec((tokens, 2 * HEAD_DIM), lambda h: (0, h))
    return pl.pallas_call(
        local_kernel,
        grid=(heads,),
        in_specs=[
            whole((tokens, width)),
            whole((tokens, width)),
            wide,
            wide,
            wide,
            pl.BlockSpec((WINDOW, HEAD_DIM), lambda h: (0, h)),
            pl.BlockSpec((WINDOW, HEAD_DIM), lambda h: (1, h)),
            whole((tokens, 1)),
            whole((1, tokens)),
            whole((1, tokens + WINDOW)),
        ],
        out_specs=[double, wide],
        out_shape=[
            jax.ShapeDtypeStruct((tokens, 2 * heads * HEAD_DIM), jnp.float32),
            jax.ShapeDtypeStruct((tokens, heads * HEAD_DIM), jnp.float32),
        ],
        compiler_params=pltpu.CompilerParams(vmem_limit_bytes=28 << 20),
        cost_estimate=pl.CostEstimate(
            flops=heads * tokens * tokens * 1536,
            bytes_accessed=20 << 20,
            transcendentals=heads * tokens * 192,
        ),
        name="mix_local",
    )(fq, fk, q, k, v, tail, tail, seg_col, seg_row, key_seg)


def mix_carry(fq, seg_col, carried, state, normal, tables, sums, near):
    tokens, width = fq.shape
    heads = near.shape[1] // HEAD_DIM
    first, second, rows, _ = tables
    per_head = pl.BlockSpec((1, ROWS, width), lambda h: (h, 0, 0))
    wide = pl.BlockSpec((tokens, HEAD_DIM), lambda h: (0, h))
    double = pl.BlockSpec((tokens, 2 * HEAD_DIM), lambda h: (0, h))
    return pl.pallas_call(
        carry_kernel,
        grid=(heads,),
        in_specs=[
            whole((tokens, width)),
            whole((tokens, 1)),
            whole((1, HEAD_DIM)),
            pl.BlockSpec((1, ROWS, HEAD_DIM), lambda h: (h, 0, 0)),
            whole((ROWS, HEAD_DIM)),
            per_head,
            per_head,
            whole((8, ROWS)),
            double,
            wide,
        ],
        out_specs=wide,
        out_shape=jax.ShapeDtypeStruct((tokens, heads * HEAD_DIM), jnp.bfloat16),
        compiler_params=pltpu.CompilerParams(vmem_limit_bytes=28 << 20),
        cost_estimate=pl.CostEstimate(
            flops=heads * tokens * 160 * 1024, bytes_accessed=16 << 20, transcendentals=0
        ),
        name="mix_carry",
    )(fq, seg_col, carried, state, normal, first, second, rows, sums, near)


def body(tokens, segment, w_feat_q, w_feat_k, w_query, w_key, w_value, w_out):
    group = lax.axis_size("tp")
    chips = group // CORES
    ranges = lax.axis_size("ctx")
    place = lax.axis_index("ctx")
    me = lax.axis_index("tp")
    chip, core = me // CORES, me % CORES
    part = tokens.shape[0]
    pair_rows = CORES * part
    count = segment.shape[0]
    heads = w_value.shape[1] // HEAD_DIM
    tables = feature_tables(heads)

    swap = [(i, i ^ 1) for i in range(group)]

    def to_chip(block, distance):
        return lax.ppermute(
            block, "tp", [(i, (i + CORES * distance) % group) for i in range(group)]
        )

    onward = [(i, i + 1) for i in range(ranges - 1)]
    seg_float = segment.astype(jnp.float32)
    tail_mark = lax.ppermute(segment[-WINDOW:] + 1, "ctx", onward).astype(jnp.float32)
    last = seg_float[-1]
    seg_row, seg_col = seg_float[None, :], seg_float[:, None]
    key_seg = jnp.concatenate([tail_mark, seg_float + 1.0])[None, :]

    def pair_of(block):
        other = lax.ppermute(block, "tp", swap)
        low = jnp.where(core == 0, block, other)
        high = jnp.where(core == 0, other, block)
        return jnp.concatenate([low, high], axis=0)

    arriving = [to_chip(tokens, r) for r in range(1, chips)]
    weights = (w_value, w_feat_k, w_key, w_query, w_feat_q)

    def placed(results, piece, distance):
        at = lax.rem(chip + chips - distance, chips) * pair_rows
        return [
            lax.dynamic_update_slice(
                result,
                jnp.dot(piece, weight, preferred_element_type=jnp.float32).astype(jnp.bfloat16),
                (at, 0),
            )
            for result, weight in zip(results, weights)
        ]

    results = [jnp.zeros((count, weight.shape[1]), jnp.bfloat16) for weight in weights]
    results = placed(results, pair_of(tokens), 0)
    for r, block in enumerate(arriving, 1):
        block, results = lax.optimization_barrier((block, results))
        results = placed(results, pair_of(block), r)
    value, feat_k, key, query, feat_q = results
    last_lanes = jnp.full((1, HEAD_DIM), last)
    payload = own_state(feat_k, value, seg_row, last_lanes, tables)
    everything = lax.all_gather(payload, "ctx")
    tail = lax.ppermute(
        jnp.concatenate([key[-WINDOW:], value[-WINDOW:]], axis=0), "ctx", onward
    )

    sums, near = mix_local(
        feat_q, feat_k, query, key, value, tail, seg_col, seg_row, key_seg
    )
    everything, sums = lax.optimization_barrier((everything, sums))

    marks = everything[:, heads, ROWS - 1, MARK_LANE].astype(jnp.float32)
    order = jnp.arange(ranges)
    carried = jnp.max(jnp.where(order < place, marks, -5.0))
    chosen = (order < place) & (marks == carried)
    summed = jnp.sum(
        jnp.where(chosen[:, None, None, None], everything.astype(jnp.float32), 0.0), axis=0
    )
    state = summed[:heads]
    normal = summed[heads, :, :LOW_LANE] + summed[heads, :, LOW_LANE:]
    normal = jnp.concatenate([normal, normal], axis=1)
    mixed = mix_carry(
        feat_q, seg_col, jnp.full((1, HEAD_DIM), carried), state, normal, tables, sums, near
    )

    def partial_sum(mixed, to, which):
        rows = lax.dynamic_slice(
            mixed, (to * pair_rows + which * part, 0), (part, mixed.shape[1])
        )
        return jnp.dot(rows, w_out, preferred_element_type=jnp.float32)

    def chip_sum(mixed, to):
        mine_to_give = partial_sum(mixed, to, 1 - core).astype(jnp.bfloat16)
        given = lax.ppermute(mine_to_give, "tp", swap)
        mixed, mine_to_give = lax.optimization_barrier((mixed, mine_to_give))
        kept = lax.optimization_barrier(partial_sum(mixed, to, core))
        return kept + given.astype(jnp.float32)

    received = []
    for r in range(1, chips):
        outgoing = chip_sum(mixed, lax.rem(chip + r, chips)).astype(jnp.bfloat16)
        received.append(to_chip(outgoing, r))
        mixed, outgoing = lax.optimization_barrier((mixed, outgoing))
    total = chip_sum(mixed, chip)
    if received:
        total, *received = lax.optimization_barrier((total, *received))
    for block in received:
        total = total + block.astype(jnp.float32)
    return total.astype(jnp.bfloat16)


def solution(mesh):
    in_specs = (
        P(("ctx", "tp"), None),
        P("ctx"),
        P(None, "tp"),
        P(None, "tp"),
        P(None, "tp"),
        P(None, "tp"),
        P(None, "tp"),
        P("tp", None),
    )
    out_specs = P(("ctx", "tp"), None)
    return jax.shard_map(body, mesh=mesh, in_specs=in_specs, out_specs=out_specs, check_vma=False)
```

```python
import functools

import jax
import jax.numpy as jnp
import numpy as np
from jax import lax
from jax.experimental import pallas as pl
from jax.experimental.pallas import tpu as pltpu
from jax.sharding import PartitionSpec as P

HEAD_DIM = 128
FEAT = 16
WINDOW = 64
CORES = 2
ROWS = 160
MARK_LANE = 127
LOW_LANE = 64


def feature_tables(heads):
    first = np.zeros((heads, ROWS, heads * FEAT), np.float32)
    second = np.zeros((heads, ROWS, heads * FEAT), np.float32)
    rows = np.zeros((8, ROWS), np.float32)
    rows[0, 0] = rows[1, 0] = rows[2, 0] = 1.0
    for i in range(FEAT):
        rows[1, 1 + i] = 1.0
        rows[2, 1 + i] = 0.25
        for h in range(heads):
            first[h, 1 + i, h * FEAT + i] = 1.0
    at = 1 + FEAT
    for i in range(FEAT):
        for j in range(i, FEAT):
            rows[2, at] = 1.0 / 32 if i == j else 1.0 / 16
            for h in range(heads):
                first[h, at, h * FEAT + i] = 1.0
                second[h, at, h * FEAT + j] = 1.0
            at += 1
    return (
        jnp.asarray(first, jnp.bfloat16),
        jnp.asarray(second, jnp.bfloat16),
        jnp.asarray(rows),
        jnp.asarray(np.ascontiguousarray(rows.T)),
    )


def dot_last(a, b):
    return lax.dot_general(a, b, (((1,), (1,)), ((), ())), preferred_element_type=jnp.float32)


def dot_f32(a, b):
    return jnp.dot(a, b, preferred_element_type=jnp.float32)


def state_kernel(heads, fk, v, seg_row, last, first, second, cols, out):
    h = pl.program_id(0)
    keep = (seg_row[...] == last[:, :1]).astype(jnp.float32)
    a = dot_last(first[0], fk[...]) + cols[:, 0:1]
    b = dot_last(second[0], fk[...]) + cols[:, 1:2]
    phi = (a * b * keep).astype(jnp.bfloat16)
    out[pl.ds(h, 1)] = dot_f32(phi, v[...]).astype(jnp.bfloat16)[None]
    normal = jnp.sum(phi.astype(jnp.float32), axis=1, keepdims=True)
    high = normal.astype(jnp.bfloat16).astype(jnp.float32)
    low = normal - high
    lane = lax.broadcasted_iota(jnp.int32, (ROWS, HEAD_DIM), 1)
    row = lax.broadcasted_iota(jnp.int32, (ROWS, HEAD_DIM), 0)

    @pl.when(h == 0)
    def _():
        mark = jnp.where((row == ROWS - 1) & (lane == MARK_LANE), last[:, :1], 0.0)
        out[heads] = mark.astype(jnp.bfloat16)

    add = jnp.where(lane == h, high, jnp.where(lane == h + LOW_LANE, low, 0.0))
    out[heads] = (out[heads].astype(jnp.float32) + add).astype(jnp.bfloat16)


def local_kernel(
    fq, fk, q, k, v, tail_k, tail_v, seg_col, seg_row, key_seg, sums, near_out,
):
    h = pl.program_id(0)
    tokens, width = fq.shape
    lane = lax.broadcasted_iota(jnp.int32, (1, width), 1)
    mine = ((lane >= h * FEAT) & (lane < (h + 1) * FEAT)).astype(jnp.float32)
    fk_head = fk[...] * mine.astype(jnp.bfloat16)
    fq_scaled = fq[...] * jnp.asarray(0.25, jnp.bfloat16)
    value = jnp.concatenate([v[...], jnp.ones((tokens, HEAD_DIM), jnp.bfloat16)], axis=1)
    tail = jnp.concatenate([tail_v[...], jnp.ones((WINDOW, HEAD_DIM), jnp.bfloat16)], axis=1)

    block = min(256, tokens)
    for begin in range(0, tokens, block):
        finish = begin + block
        seg_here = seg_col[begin:finish]
        total = None
        if begin:
            inner = dot_last(fq_scaled[begin:finish], fk_head[:begin]) + 1.0
            kernel = jnp.where(
                seg_here == seg_row[:, :begin], 0.5 * (inner * inner) + 0.5, 0.0
            )
            total = dot_f32(kernel.astype(jnp.bfloat16), value[:begin])
        inner = dot_last(fq_scaled[begin:finish], fk_head[begin:finish]) + 1.0
        row_at = lax.broadcasted_iota(jnp.int32, (block, block), 0)
        col_at = lax.broadcasted_iota(jnp.int32, (block, block), 1)
        kernel = jnp.where(
            (seg_here == seg_row[:, begin:finish]) & (col_at <= row_at),
            0.5 * (inner * inner) + 0.5,
            0.0,
        )
        here = dot_f32(kernel.astype(jnp.bfloat16), value[begin:finish])
        sums[begin:finish] = here if total is None else total + here

        small = min(128, block)
        for start in range(begin, finish, small):
            stop = start + small
            if start:
                keys, values = k[start - WINDOW : stop], value[start - WINDOW : stop]
            else:
                keys = jnp.concatenate([tail_k[...], k[:stop]], axis=0)
                values = jnp.concatenate([tail, value[:stop]], axis=0)
            scores = dot_last(q[start:stop], keys) * (1.4426950408889634 / HEAD_DIM**0.5)
            row_at = lax.broadcasted_iota(jnp.int32, (small, small + WINDOW), 0)
            col_at = lax.broadcasted_iota(jnp.int32, (small, small + WINDOW), 1)
            near = (col_at <= row_at + WINDOW) & (col_at > row_at)
            same = key_seg[:, start : stop + WINDOW] == seg_col[start:stop] + 1.0
            scores = jnp.where(near & same, scores, -jnp.inf)
            peak = jnp.max(scores, axis=1, keepdims=True)
            expo = jnp.exp2(scores - peak).astype(jnp.bfloat16)
            near_sum = dot_f32(expo, values)
            part = near_sum[:, :HEAD_DIM] / near_sum[:, HEAD_DIM:]
            near_out[start:stop] = part


def carry_kernel(fq, seg_col, carried, state, normal, first, second, rows, sums, near_in, out):
    h = pl.program_id(0)
    tokens = fq.shape[0]
    state_lane = lax.broadcasted_iota(jnp.int32, (ROWS, HEAD_DIM), 1)
    column = jnp.sum(jnp.where(state_lane == h, normal[...], 0.0), axis=1, keepdims=True)
    joint = jnp.concatenate([state[0], jnp.broadcast_to(column, (ROWS, HEAD_DIM))], axis=1)
    joint_high = joint.astype(jnp.bfloat16)
    joint_low = (joint - joint_high.astype(jnp.float32)).astype(jnp.bfloat16)
    block = min(256, tokens)
    for begin in range(0, tokens, block):
        finish = begin + block
        a = dot_last(fq[begin:finish], first[0]) + rows[0:1]
        b = dot_last(fq[begin:finish], second[0]) + rows[1:2]
        phi = (a * b * rows[2:3]).astype(jnp.bfloat16)
        entering = dot_f32(phi, joint_high) + dot_f32(phi, joint_low)
        total = sums[begin:finish] + jnp.where(
            seg_col[begin:finish] == carried[:, :1], entering, 0.0
        )
        linear = total[:, :HEAD_DIM] / total[:, HEAD_DIM:]
        out[begin:finish] = (linear + near_in[begin:finish]).astype(jnp.bfloat16)


def whole(shape):
    return pl.BlockSpec(shape, lambda h: (0,) * len(shape))


def own_state(fk, v, seg_row, last, tables):
    tokens, width = fk.shape
    heads = v.shape[1] // HEAD_DIM
    first, second, _, cols = tables
    per_head = pl.BlockSpec((1, ROWS, width), lambda h: (h, 0, 0))
    return pl.pallas_call(
        functools.partial(state_kernel, heads),
        grid=(heads,),
        in_specs=[
            whole((tokens, width)),
            pl.BlockSpec((tokens, HEAD_DIM), lambda h: (0, h)),
            whole((1, tokens)),
            whole((1, HEAD_DIM)),
            per_head,
            per_head,
            whole((ROWS, 8)),
        ],
        out_specs=whole((heads + 1, ROWS, HEAD_DIM)),
        out_shape=jax.ShapeDtypeStruct((heads + 1, ROWS, HEAD_DIM), jnp.bfloat16),
        compiler_params=pltpu.CompilerParams(vmem_limit_bytes=32 << 20),
        cost_estimate=pl.CostEstimate(
            flops=2 * heads * ROWS * tokens * 384, bytes_accessed=4 << 20, transcendentals=0
        ),
        name="own_state",
    )(fk, v, seg_row, last, first, second, cols)


def mix_local(fq, fk, q, k, v, tail, seg_col, seg_row, key_seg):
    tokens, width = fk.shape
    heads = v.shape[1] // HEAD_DIM
    wide = pl.BlockSpec((tokens, HEAD_DIM), lambda h: (0, h))
    double = pl.BlockSpec((tokens, 2 * HEAD_DIM), lambda h: (0, h))
    return pl.pallas_call(
        local_kernel,
        grid=(heads,),
        in_specs=[
            whole((tokens, width)),
            whole((tokens, width)),
            wide,
            wide,
            wide,
            pl.BlockSpec((WINDOW, HEAD_DIM), lambda h: (0, h)),
            pl.BlockSpec((WINDOW, HEAD_DIM), lambda h: (1, h)),
            whole((tokens, 1)),
            whole((1, tokens)),
            whole((1, tokens + WINDOW)),
        ],
        out_specs=[double, wide],
        out_shape=[
            jax.ShapeDtypeStruct((tokens, 2 * heads * HEAD_DIM), jnp.float32),
            jax.ShapeDtypeStruct((tokens, heads * HEAD_DIM), jnp.float32),
        ],
        compiler_params=pltpu.CompilerParams(vmem_limit_bytes=28 << 20),
        cost_estimate=pl.CostEstimate(
            flops=heads * tokens * tokens * 1536,
            bytes_accessed=20 << 20,
            transcendentals=heads * tokens * 192,
        ),
        name="mix_local",
    )(fq, fk, q, k, v, tail, tail, seg_col, seg_row, key_seg)


def mix_carry(fq, seg_col, carried, state, normal, tables, sums, near):
    tokens, width = fq.shape
    heads = near.shape[1] // HEAD_DIM
    first, second, rows, _ = tables
    per_head = pl.BlockSpec((1, ROWS, width), lambda h: (h, 0, 0))
    wide = pl.BlockSpec((tokens, HEAD_DIM), lambda h: (0, h))
    double = pl.BlockSpec((tokens, 2 * HEAD_DIM), lambda h: (0, h))
    return pl.pallas_call(
        carry_kernel,
        grid=(heads,),
        in_specs=[
            whole((tokens, width)),
            whole((tokens, 1)),
            whole((1, HEAD_DIM)),
            pl.BlockSpec((1, ROWS, HEAD_DIM), lambda h: (h, 0, 0)),
            whole((ROWS, HEAD_DIM)),
            per_head,
            per_head,
            whole((8, ROWS)),
            double,
            wide,
        ],
        out_specs=wide,
        out_shape=jax.ShapeDtypeStruct((tokens, heads * HEAD_DIM), jnp.bfloat16),
        compiler_params=pltpu.CompilerParams(vmem_limit_bytes=28 << 20),
        cost_estimate=pl.CostEstimate(
            flops=heads * tokens * 160 * 1024, bytes_accessed=16 << 20, transcendentals=0
        ),
        name="mix_carry",
    )(fq, seg_col, carried, state, normal, first, second, rows, sums, near)


def body(tokens, segment, w_feat_q, w_feat_k, w_query, w_key, w_value, w_out):
    group = lax.axis_size("tp")
    chips = group // CORES
    ranges = lax.axis_size("ctx")
    place = lax.axis_index("ctx")
    me = lax.axis_index("tp")
    chip, core = me // CORES, me % CORES
    part = tokens.shape[0]
    pair_rows = CORES * part
    count = segment.shape[0]
    heads = w_value.shape[1] // HEAD_DIM
    tables = feature_tables(heads)

    swap = [(i, i ^ 1) for i in range(group)]

    def to_chip(block, distance):
        return lax.ppermute(
            block, "tp", [(i, (i + CORES * distance) % group) for i in range(group)]
        )

    onward = [(i, i + 1) for i in range(ranges - 1)]
    seg_float = segment.astype(jnp.float32)
    tail_mark = lax.ppermute(segment[-WINDOW:] + 1, "ctx", onward).astype(jnp.float32)
    last = seg_float[-1]
    seg_row, seg_col = seg_float[None, :], seg_float[:, None]
    key_seg = jnp.concatenate([tail_mark, seg_float + 1.0])[None, :]

    def pair_of(block):
        other = lax.ppermute(block, "tp", swap)
        low = jnp.where(core == 0, block, other)
        high = jnp.where(core == 0, other, block)
        return jnp.concatenate([low, high], axis=0)

    arriving = [to_chip(tokens, r) for r in range(1, chips)]
    weights = (w_value, w_feat_k, w_key, w_query, w_feat_q)

    def placed(results, piece, distance):
        at = lax.rem(chip + chips - distance, chips) * pair_rows
        return [
            lax.dynamic_update_slice(
                result,
                jnp.dot(piece, weight, preferred_element_type=jnp.float32).astype(jnp.bfloat16),
                (at, 0),
            )
            for result, weight in zip(results, weights)
        ]

    results = [jnp.zeros((count, weight.shape[1]), jnp.bfloat16) for weight in weights]
    results = placed(results, pair_of(tokens), 0)
    for r, block in enumerate(arriving, 1):
        block, results = lax.optimization_barrier((block, results))
        results = placed(results, pair_of(block), r)
    value, feat_k, key, query, feat_q = results
    last_lanes = jnp.full((1, HEAD_DIM), last)
    payload = own_state(feat_k, value, seg_row, last_lanes, tables)
    everything = lax.all_gather(payload, "ctx")
    tail = lax.ppermute(
        jnp.concatenate([key[-WINDOW:], value[-WINDOW:]], axis=0), "ctx", onward
    )

    sums, near = mix_local(
        feat_q, feat_k, query, key, value, tail, seg_col, seg_row, key_seg
    )

    block_at = jnp.arange(ROWS)[:, None] * HEAD_DIM + jnp.arange(HEAD_DIM)[None, :]
    at_mark = block_at == (ROWS - 1) * HEAD_DIM + MARK_LANE
    marks = jnp.max(
        jnp.where(at_mark, everything[:, heads].astype(jnp.float32), -5.0), axis=(1, 2)
    )
    order = jnp.arange(ranges)
    carried = jnp.max(jnp.where(order < place, marks, -5.0))
    chosen = (order < place) & (marks == carried)
    summed = jnp.sum(
        jnp.where(chosen[:, None, None, None], everything.astype(jnp.float32), 0.0), axis=0
    )
    state = summed[:heads]
    normal = summed[heads, :, :LOW_LANE] + summed[heads, :, LOW_LANE:]
    normal = jnp.concatenate([normal, normal], axis=1)
    mixed = mix_carry(
        feat_q, seg_col, jnp.full((1, HEAD_DIM), carried), state, normal, tables, sums, near
    )

    def partial_sum(mixed, to, which):
        rows = lax.dynamic_slice(
            mixed, (to * pair_rows + which * part, 0), (part, mixed.shape[1])
        )
        return jnp.dot(rows, w_out, preferred_element_type=jnp.float32)

    def chip_sum(mixed, to):
        mine_to_give = partial_sum(mixed, to, 1 - core).astype(jnp.bfloat16)
        given = lax.ppermute(mine_to_give, "tp", swap)
        mixed, mine_to_give = lax.optimization_barrier((mixed, mine_to_give))
        kept = lax.optimization_barrier(partial_sum(mixed, to, core))
        return kept + given.astype(jnp.float32)

    received = []
    for r in range(1, chips):
        outgoing = chip_sum(mixed, lax.rem(chip + r, chips)).astype(jnp.bfloat16)
        received.append(to_chip(outgoing, r))
        mixed, outgoing = lax.optimization_barrier((mixed, outgoing))
    total = chip_sum(mixed, chip)
    if received:
        total, *received = lax.optimization_barrier((total, *received))
    for block in received:
        total = total + block.astype(jnp.float32)
    return total.astype(jnp.bfloat16)


def solution(mesh):
    in_specs = (
        P(("ctx", "tp"), None),
        P("ctx"),
        P(None, "tp"),
        P(None, "tp"),
        P(None, "tp"),
        P(None, "tp"),
        P(None, "tp"),
        P("tp", None),
    )
    out_specs = P(("ctx", "tp"), None)
    return jax.shard_map(body, mesh=mesh, in_specs=in_specs, out_specs=out_specs, check_vma=False)
```
